512 devices in a mesh: replica: 8 (over y, core), expert: 8 (over z_hi, x), fsdp: 8 (over z_lo).
Axes of the slice: x: 4, y: 4, z: 16 (z_hi: 2, z_lo: 8; z = z_hi * 8 + z_lo), core: 2. Of those that a mesh axis runs over, the one named last changes fastest.
Arguments:
- out_grad: bfloat16 [65536, 6144], P(('replica', 'expert', 'fsdp')), may hold values from -6 to 6
- saved_out: bfloat16 [8, 8, 8, 8, 34, 6144], P('replica', 'expert', 'fsdp'), may hold values from -6 to 6
- top_logits: float32 [65536, 2], P(('replica', 'expert', 'fsdp')), may hold values from -8 to 8
- expert_ids: int32 [65536, 2], P(('replica', 'expert', 'fsdp')), may hold values from 0 to 7, all different within a row; in each aligned block of 128 rows (0 to 127, 128 to 255, ...) at most 34 rows name the same one
- outer_params: float32 [128, 6144], P(('expert', 'fsdp')), may hold values from -6 to 6
- local_params: float32 [8, 128, 6144], P('replica', ('expert', 'fsdp')), may hold values from -6 to 6
- momentum: float32 [128, 6144], P(('expert', 'fsdp')), may hold values from -4 to 4
- fragment: int32 [8], P('replica'), may hold values from 0 to 3
- mix_rates: float32 [4], replicated, may hold values from 0.2 to 0.8
Outputs:
- logit_grad: float32 [65536, 2], P(('replica', 'expert', 'fsdp'))
- new_outer: float32 [128, 6144], P(('expert', 'fsdp'))
- new_momentum: float32 [128, 6144], P(('expert', 'fsdp'))
- mixed_params: float32 [8, 128, 6144], P('replica', ('expert', 'fsdp'))
The draws below stay inside these ranges and needn't reach their ends.
Inputs may be any that keep to these rules, and one draw needn't show every extreme that they name: `expert_ids`: in each aligned block of 128 rows (the rows of one device) no expert is named by more than 34 rows, a bound that some block reaches; the two experts of a row differ.
All inputs are finite; a program needn't handle non-finite values.
Results may differ from the reference program's by a relative error of at most 0.0022.
The reference program's roundings to bfloat16 on the way (of `payload`) count: a program that leaves them out, or rounds other values in their place, can miss the bound.
Values may be sent and summed in bfloat16 or wider, within the bound.
No kernel may reach another device: no remote copies, remote signals or barrier semaphores. Data moves between devices by JAX's collectives and lax.ppermute only.
A program may use at most 64 MiB of HBM per device.

```python
import math
import jax
import jax.numpy as jnp
import numpy as np
from jax import lax

D = 6144
EXPERTS = 8
TOP = 2
TOK_DEV = 128
FRAGS = 4
CAP = 34
TOKENS = 65536
FRAG_ROWS = 128
N_REPLICA = 8
N_EXPERT = 8
N_FSDP = 8


def with_ends(values, rng, low, largest):
    dims = values.shape
    index_at = [jax.random.randint(jax.random.fold_in(rng, axis), (), 0, dims[axis]) for axis in range(len(dims))]
    values = values.at[tuple(index_at)].set(low)
    longest = dims.index(max(dims))
    index_at[longest] = (index_at[longest] + 1) % dims[longest]
    return values.at[tuple(index_at)].set(largest)


def level_of(stream_key, extent, split, least, largest):
    def one(dim, parts):
        steps = jax.random.uniform(jax.random.fold_in(jax.random.fold_in(stream_key, 6), dim), (parts,), jnp.float32, least / len(split), largest / len(split))
        return jnp.repeat(jnp.exp(steps), extent[dim] // parts).reshape((-1,) + (1,) * (len(extent) - dim - 1))

    level = one(*split[0])
    for cut in split[1:]:
        level = level * one(*cut)
    return level


def assign_block(key, own, number, rows, count, top, most, slope):
    ranking = jax.random.permutation(key, count)
    packed, ordinary = load_shares(count, rows * top, most, slope, True), load_shares(count, rows * top, most, slope, False)
    places = jnp.arange(count)

    def named(sizes, rotation):
        used = int((sizes > 0).sum())
        fixed = max(1, used // 4)
        moved = fixed + (places - fixed + rotation * (used - fixed)) % max(1, count - fixed)
        return jnp.zeros((count,), jnp.int32).at[ranking[jnp.where(places < fixed, places, moved)]].set(jnp.asarray(sizes, jnp.int32))

    sizes = jnp.where(number % 4 == 0, named(packed, number // 4), named(ordinary, number - number // 4 - 1))
    mixed = jax.random.permutation(jax.random.fold_in(own, 3), count)
    source_of, taker = mixed[0:count // 2 * 2:2], mixed[1:count // 2 * 2:2]
    room = jnp.minimum(sizes[source_of] - 1, most - sizes[taker]) // 2
    room = jnp.where((source_of == ranking[0]) | (taker == ranking[0]) | (sizes[taker] == 0), 0, jnp.maximum(room, 0))
    moved = jax.random.randint(jax.random.fold_in(own, 4), (count // 2,), 0, 1 << 20) % (room + 1)
    sizes = sizes.at[source_of].add(-moved).at[taker].add(moved)
    items = jnp.searchsorted(jnp.cumsum(sizes), jnp.arange(rows * top), side="right").astype(jnp.int32)
    listing = items.reshape(top, rows).T
    listing = listing[jax.random.permutation(jax.random.fold_in(own, 1), rows)]
    rotation = jax.random.randint(jax.random.fold_in(own, 2), (rows, 1), 0, top)
    return jnp.take_along_axis(listing, (jnp.arange(top)[None, :] + rotation) % top, axis=1)


def load_shares(number_of, total, most, slope, full):
    portions = [(1 << 20) // math.isqrt(standing ** slope) + 1 for standing in range(1, number_of + 1)]
    largest = most if full else min(most, max(-(-total // number_of), total * portions[0] // sum(portions)))
    least = 1 if total - largest >= number_of - 1 else 0
    given, surplus = [largest] + [least] * (number_of - 1), total - largest - least * (number_of - 1)
    while surplus > 0:
        movable = [i for i in range(1, number_of) if given[i] < largest] or [i for i in range(1, number_of) if given[i] < most]
        mass, budget = sum([portions[i] for i in movable]), surplus
        for i in movable:
            addition = min(most - given[i], max(1, budget * portions[i] // mass), surplus)
            given[i] = given[i] + addition
            surplus = surplus - addition
    return np.array(given)


def normal_values(stream_key, extent, width, most, cuts=(), kind=jnp.bfloat16):
    entries = jax.random.normal(stream_key, extent, jnp.float32) * width
    if len(cuts) > 0:
        entries = level_of(stream_key, extent, cuts, -0.22, 0.18) * entries
    return jnp.clip(entries, min=-most, max=most).astype(kind)


def setup_inputs(seed: int = 0) -> dict:
    streams_of = jax.random.split(jax.random.key(seed), 10)
    out_grad = normal_values(streams_of[0], (TOKENS, D), 1.0, 6.0, ((0, 512),))
    saved_out = normal_values(streams_of[1], (N_REPLICA, EXPERTS, N_FSDP, N_EXPERT, CAP, D), 1.0, 6.0, ((0, 8), (1, 8), (2, 8)))
    top_logits = normal_values(streams_of[2], (TOKENS, TOP), 2.0, 8.0, ((0, 512),), jnp.float32)
    expert_ids_keys = jax.random.split(jax.random.fold_in(streams_of[3], 1), TOKENS // TOK_DEV)
    expert_ids_turns = jax.random.permutation(jax.random.fold_in(streams_of[3], 3), TOKENS // TOK_DEV)
    expert_ids = jax.vmap(lambda own, number: assign_block(jax.random.fold_in(streams_of[3], 2), own, number, TOK_DEV, EXPERTS, TOP, CAP, 2))(expert_ids_keys, expert_ids_turns).reshape((TOKENS, TOP))
    outer_params = normal_values(streams_of[4], (FRAG_ROWS, D), 1.0, 6.0, ((0, 64),), jnp.float32)
    local_params = normal_values(streams_of[5], (N_REPLICA, FRAG_ROWS, D), 1.0, 6.0, ((0, 8), (1, 64)), jnp.float32)
    momentum = normal_values(streams_of[6], (FRAG_ROWS, D), 0.5, 4.0, ((0, 64),), jnp.float32)
    fragment = with_ends(jax.random.randint(streams_of[7], (N_REPLICA,), 0, FRAGS), jax.random.fold_in(streams_of[7], 1), 0, FRAGS - 1).astype(jnp.int32)
    mix_rates = jnp.clip(jax.random.uniform(streams_of[8], (FRAGS,), jnp.float32, 0.2, 0.8), 0.2, 0.8)
    return dict(out_grad=out_grad, saved_out=saved_out, top_logits=top_logits, expert_ids=expert_ids, outer_params=outer_params, local_params=local_params, momentum=momentum, fragment=fragment, mix_rates=mix_rates)


def group_grad(grads, saved, logits, ids):
    flat_ids = ids.reshape(-1)
    onehot = (flat_ids[:, None] == jnp.arange(EXPERTS, dtype=jnp.int32)[None, :]).astype(jnp.int32)
    position = lax.optimization_barrier(jnp.sum((jnp.cumsum(onehot, axis=0) - 1) * onehot, axis=1))
    slot_index = flat_ids * CAP + position
    lanes = jnp.arange(EXPERTS * CAP, dtype=jnp.int32)
    dispatch = (slot_index[None, :] == lanes[:, None]).astype(jnp.bfloat16)
    first = jax.nn.sigmoid(logits[:, 0] - logits[:, 1])
    probs = jnp.stack([first, 1.0 - first], axis=1)
    scaled = (probs[:, :, None] * grads[:, None, :].astype(jnp.float32)).astype(jnp.bfloat16)
    scaled = scaled.reshape(TOK_DEV * TOP, D)
    payload = jnp.dot(dispatch, scaled, preferred_element_type=jnp.float32).astype(jnp.bfloat16)
    payload = payload.reshape(EXPERTS, CAP, D)
    products = jnp.einsum('ecd,ecd->ec', payload.astype(jnp.float32), saved.astype(jnp.float32)).reshape(-1)
    pair = jnp.take(products, slot_index).reshape(TOK_DEV, TOP)
    return pair - probs * lax.optimization_barrier(jnp.sum(pair, axis=1, keepdims=True))

def reference(out_grad, saved_out, top_logits, expert_ids, outer_params, local_params, momentum, fragment, mix_rates):
    groups = N_REPLICA * N_EXPERT * N_FSDP
    grads = out_grad.reshape(groups, TOK_DEV, D)
    ids = expert_ids.reshape(groups, TOK_DEV, TOP)
    logits = top_logits.reshape(groups, TOK_DEV, TOP)

    def one(index):
        rep = index // (N_EXPERT * N_FSDP)
        src = index // N_FSDP % N_EXPERT
        shard = index % N_FSDP
        block = lax.dynamic_index_in_dim(saved_out, rep, 0, False)
        block = lax.dynamic_index_in_dim(block, shard, 1, False)
        block = lax.dynamic_index_in_dim(block, src, 1, False)
        return group_grad(grads[index], block, logits[index], ids[index])
    logit_grad = lax.map(one, jnp.arange(groups, dtype=jnp.int32)).reshape(TOKENS, TOP)
    pseudo = lax.optimization_barrier(jnp.sum(outer_params[None] - local_params, axis=0)) / N_REPLICA
    total_sq = jnp.sum(pseudo * pseudo)
    limit = 0.25 * jnp.sqrt(jnp.float32(FRAG_ROWS * D) / N_REPLICA)
    scale = jnp.minimum(1.0, limit / jnp.sqrt(total_sq + 1e-06))
    clipped = scale * pseudo
    new_momentum = 0.9 * momentum + clipped
    new_outer = outer_params - 0.7 * (clipped + 0.9 * new_momentum)
    rate = jnp.take(mix_rates, fragment)[:, None, None]
    mixed_params = local_params + rate * (new_outer[None] - local_params)
    return (logit_grad, new_outer, new_momentum, mixed_params)
```

```python
import jax
import jax.numpy as jnp
from jax import lax
from jax.sharding import PartitionSpec as P

HEAD = 1536


def shards(
    out_grad,
    saved_out,
    top_logits,
    expert_ids,
    outer_params,
    local_params,
    momentum,
    fragment,
    mix_rates,
):
    tokens, width = out_grad.shape
    owners = lax.axis_size("expert")
    capacity = saved_out.shape[4]
    side = owners // 2
    block = side * capacity
    me = lax.axis_index("expert")
    half = me // side
    groups = [list(range(side)), list(range(side, owners))]
    across = [(e, (e + side) % owners) for e in range(owners)]

    def along_x(value):
        return lax.all_to_all(
            value, "expert", split_axis=0, concat_axis=0, axis_index_groups=groups, tiled=True
        )

    def over_z(value):
        return lax.ppermute(value, "expert", across)

    saved = saved_out.reshape(owners, capacity, width)
    far = lax.dynamic_slice_in_dim(saved, (1 - half) * side, side, 0)
    near = lax.dynamic_slice_in_dim(saved, half * side, side, 0)

    head = over_z(far[:, :, :HEAD].reshape(block, HEAD))
    rest = over_z(along_x(far[:, :, HEAD:]).reshape(block, width - HEAD))
    near_rows = along_x(near).reshape(block, width)
    head_rows = along_x(head.reshape(side, capacity, HEAD)).reshape(block, HEAD)

    count = jnp.arange(owners, dtype=jnp.int32)
    named = [(expert_ids[:, k : k + 1] == count[None, :]).astype(jnp.bfloat16) for k in range(2)]
    row = lax.broadcasted_iota(jnp.int32, (tokens, tokens), 0)
    col = lax.broadcasted_iota(jnp.int32, (tokens, tokens), 1)
    before = jnp.dot(
        (col < row).astype(jnp.bfloat16), named[0] + named[1], preferred_element_type=jnp.float32
    )
    slot = [
        expert_ids[:, k] * capacity
        + jnp.sum(before * named[k].astype(jnp.float32), axis=1).astype(jnp.int32)
        for k in range(2)
    ]
    slot = jnp.concatenate(slot)
    lanes = jnp.arange(block, dtype=jnp.int32)
    near_mask = (slot - half * block)[:, None] == lanes[None, :]
    far_mask = (slot - (1 - half) * block)[:, None] == lanes[None, :]

    first = jax.nn.sigmoid(top_logits[:, 0] - top_logits[:, 1])
    second = 1.0 - first
    grads = out_grad.astype(jnp.float32)
    payload = jnp.concatenate(
        [
            (first[:, None] * grads).astype(jnp.bfloat16),
            (second[:, None] * grads).astype(jnp.bfloat16),
        ]
    )

    def inner(a, b):
        return lax.dot_general(
            a, b, (((1,), (1,)), ((), ())), preferred_element_type=jnp.float32
        )

    near_products = jnp.where(near_mask, inner(payload, near_rows), 0.0)
    far_products = inner(payload[:, :HEAD], head_rows) + inner(payload[:, HEAD:], rest)
    pair = jnp.sum(near_products, axis=1) + jnp.sum(jnp.where(far_mask, far_products, 0.0), axis=1)
    pair0, pair1 = pair[:tokens], pair[tokens:]
    both = pair0 + pair1
    logit_grad = jnp.stack([pair0 - first * both, pair1 - second * both], axis=1)

    replicas = lax.axis_size("replica")
    pseudo = (
        lax.psum((outer_params - local_params[0]).astype(jnp.bfloat16), "replica").astype(
            jnp.float32
        )
        / replicas
    )
    total_sq = lax.psum(jnp.sum(pseudo * pseudo), ("expert", "fsdp"))
    entries = pseudo.shape[0] * lax.axis_size("expert") * lax.axis_size("fsdp") * width
    limit = 0.25 * jnp.sqrt(jnp.float32(entries) / replicas)
    scale = jnp.minimum(1.0, limit / jnp.sqrt(total_sq + 1e-06))
    clipped = scale * pseudo
    new_momentum = 0.9 * momentum + clipped
    new_outer = outer_params - 0.7 * (clipped + 0.9 * new_momentum)
    rate = jnp.take(mix_rates, fragment[0])
    mixed_params = local_params + rate * (new_outer[None] - local_params)
    return (logit_grad, new_outer, new_momentum, mixed_params)


def solution(mesh):
    in_specs = (
        P(("replica", "expert", "fsdp"), None),
        P("replica", "expert", "fsdp", None, None, None),
        P(("replica", "expert", "fsdp"), None),
        P(("replica", "expert", "fsdp"), None),
        P(("expert", "fsdp"), None),
        P("replica", ("expert", "fsdp"), None),
        P(("expert", "fsdp"), None),
        P("replica"),
        P(),
    )
    out_specs = (
        P(("replica", "expert", "fsdp"), None),
        P(("expert", "fsdp"), None),
        P(("expert", "fsdp"), None),
        P("replica", ("expert", "fsdp"), None),
    )
    return jax.shard_map(shards, mesh=mesh, in_specs=in_specs, out_specs=out_specs, check_vma=False)
```

```python
import jax
import jax.numpy as jnp
from jax import lax
from jax.sharding import PartitionSpec as P

CUTS = (0, 1536, 3072, 4096, 5120, 6144)
EARLY = 2
FLIGHT = 2
AXES = ("replica", "expert", "fsdp")


def shards(
    out_grad,
    saved_out,
    top_logits,
    expert_ids,
    outer_params,
    local_params,
    momentum,
    fragment,
    mix_rates,
):
    tokens, width = out_grad.shape
    replicas, owners, runs = (lax.axis_size(axis) for axis in AXES)
    capacity = saved_out.shape[4]
    side = owners // 2
    block = side * capacity
    half = lax.axis_index("expert") // side
    groups = [list(range(side)), list(range(side, owners))]
    across = [(e, (e + side) % owners) for e in range(owners)]

    def along_x(value):
        return lax.all_to_all(
            value, "expert", split_axis=0, concat_axis=0, axis_index_groups=groups, tiled=True
        )

    def over_z(value):
        return lax.ppermute(value, "expert", across)

    def swap_x(value, step):
        return lax.ppermute(value, "expert", [(e, e ^ step) for e in range(owners)])

    def place(r, z, x):
        return (r * owners + z // runs * side + x) * runs + z % runs

    depth = 2 * runs

    def along_z(value, start):
        return lax.ppermute(
            value,
            AXES,
            [
                (place(r, z, x), place(r, (z + start + r) % depth, x))
                for r in range(replicas)
                for z in range(depth)
                for x in range(side)
            ],
        )

    saved = saved_out.reshape(owners, capacity, width)
    other = 1 - half

    def part(which, first, last, rows=saved):
        return lax.dynamic_slice(
            rows, (which * side, 0, first), (side, capacity, last - first)
        )

    pseudo = (
        lax.psum((outer_params - local_params[0]).astype(jnp.bfloat16), "replica").astype(
            jnp.float32
        )
        / replicas
    )
    own_sq = jnp.sum(pseudo * pseudo).reshape(1, 1)
    after_sum, own_sq = lax.optimization_barrier((saved, own_sq))

    pieces = len(CUTS) - 1
    middle = EARLY + 1
    spread = {}
    for first, last in ((EARLY, middle), (middle, pieces)):
        rows = along_x(part(other, CUTS[first], CUTS[last], after_sum))
        for i in range(first, last):
            spread[i] = rows[:, :, CUTS[i] - CUTS[first] : CUTS[i + 1] - CUTS[first]]
    came = []
    for i in range(pieces):
        rows = part(other, CUTS[i], CUTS[i + 1]) if i < EARLY else spread[i]
        rows = rows.reshape(block, CUTS[i + 1] - CUTS[i])
        if i >= FLIGHT:
            rows, came[i - FLIGHT] = lax.optimization_barrier((rows, came[i - FLIGHT]))
        came.append(over_z(rows))
        if i == 0:
            came[0], own_sq = lax.optimization_barrier((came[0], own_sq))
            window = along_z(own_sq, 0) + along_z(own_sq, replicas)

    after_early, came[1], window = lax.optimization_barrier((after_sum, came[1], window))
    window = lax.psum(window, "replica")
    window = window + swap_x(window, 1)
    total_sq = (window + swap_x(window, 2))[0, 0]

    near = lax.dynamic_slice_in_dim(after_early, half * side, side, 0)
    near_rows = along_x(near).reshape(block, width)
    crossed = jnp.concatenate(came[:EARLY], axis=1).reshape(side, capacity, CUTS[EARLY])
    crossed = along_x(crossed).reshape(block, CUTS[EARLY])
    far_rows = [crossed] + came[EARLY:]
    cuts = (0,) + CUTS[EARLY:]

    count = jnp.arange(owners, dtype=jnp.int32)
    named = [(expert_ids[:, k : k + 1] == count[None, :]).astype(jnp.bfloat16) for k in range(2)]
    row = lax.broadcasted_iota(jnp.int32, (tokens, tokens), 0)
    col = lax.broadcasted_iota(jnp.int32, (tokens, tokens), 1)
    before = jnp.dot(
        (col < row).astype(jnp.bfloat16), named[0] + named[1], preferred_element_type=jnp.float32
    )
    slot = jnp.concatenate(
        [
            expert_ids[:, k] * capacity
            + jnp.sum(before * named[k].astype(jnp.float32), axis=1).astype(jnp.int32)
            for k in range(2)
        ]
    )
    lanes = jnp.arange(block, dtype=jnp.int32)
    near_mask = (slot - half * block)[:, None] == lanes[None, :]
    far_mask = (slot - other * block)[:, None] == lanes[None, :]

    first = jax.nn.sigmoid(top_logits[:, 0] - top_logits[:, 1])
    second = 1.0 - first
    grads = out_grad.astype(jnp.float32)
    payload = jnp.concatenate(
        [
            (first[:, None] * grads).astype(jnp.bfloat16),
            (second[:, None] * grads).astype(jnp.bfloat16),
        ]
    )

    def inner(a, b):
        return lax.dot_general(
            a, b, (((1,), (1,)), ((), ())), preferred_element_type=jnp.float32
        )

    def picked(mask, rows, first, last):
        return jnp.sum(jnp.where(mask, inner(payload[:, first:last], rows), 0.0), axis=1)

    pair = picked(near_mask, near_rows, 0, width)
    for i, rows in enumerate(far_rows):
        if i == len(far_rows) - 1:
            rows, pair = lax.optimization_barrier((rows, pair))
        pair = pair + picked(far_mask, rows, cuts[i], cuts[i + 1])
    pair0, pair1 = pair[:tokens], pair[tokens:]
    both = pair0 + pair1
    logit_grad = jnp.stack([pair0 - first * both, pair1 - second * both], axis=1)

    entries = pseudo.shape[0] * owners * runs * width
    limit = 0.25 * jnp.sqrt(jnp.float32(entries) / replicas)
    scale = jnp.minimum(1.0, limit / jnp.sqrt(total_sq + 1e-06))
    clipped = scale * pseudo
    new_momentum = 0.9 * momentum + clipped
    new_outer = outer_params - 0.7 * (clipped + 0.9 * new_momentum)
    rate = jnp.take(mix_rates, fragment[0])
    mixed_params = local_params + rate * (new_outer[None] - local_params)
    return (logit_grad, new_outer, new_momentum, mixed_params)


def solution(mesh):
    in_specs = (
        P(("replica", "expert", "fsdp"), None),
        P("replica", "expert", "fsdp", None, None, None),
        P(("replica", "expert", "fsdp"), None),
        P(("replica", "expert", "fsdp"), None),
        P(("expert", "fsdp"), None),
        P("replica", ("expert", "fsdp"), None),
        P(("expert", "fsdp"), None),
        P("replica"),
        P(),
    )
    out_specs = (
        P(("replica", "expert", "fsdp"), None),
        P(("expert", "fsdp"), None),
        P(("expert", "fsdp"), None),
        P("replica", ("expert", "fsdp"), None),
    )
    return jax.shard_map(shards, mesh=mesh, in_specs=in_specs, out_specs=out_specs, check_vma=False)
```

```python
import jax
import jax.numpy as jnp
from jax import lax
from jax.sharding import PartitionSpec as P

HEAD = 1536
AXES = ("replica", "expert", "fsdp")


def shards(
    out_grad,
    saved_out,
    top_logits,
    expert_ids,
    outer_params,
    local_params,
    momentum,
    fragment,
    mix_rates,
):
    tokens, width = out_grad.shape
    replicas, owners, runs = (lax.axis_size(axis) for axis in AXES)
    capacity = saved_out.shape[4]
    side = owners // 2
    block = side * capacity
    half = lax.axis_index("expert") // side
    groups = [list(range(side)), list(range(side, owners))]
    across = [(e, (e + side) % owners) for e in range(owners)]

    def along_x(value):
        return lax.all_to_all(
            value, "expert", split_axis=0, concat_axis=0, axis_index_groups=groups, tiled=True
        )

    def over_z(value):
        return lax.ppermute(value, "expert", across)

    def swap_x(value, step):
        return lax.ppermute(value, "expert", [(e, e ^ step) for e in range(owners)])

    def place(r, z, x):
        return (r * owners + z // runs * side + x) * runs + z % runs

    depth = 2 * runs

    def along_z(value):
        return lax.ppermute(
            value,
            AXES,
            [
                (place(r, z, x), place(r, (z + r + x // 2 * replicas) % depth, x))
                for r in range(replicas)
                for z in range(depth)
                for x in range(side)
            ],
        )

    def tie(*values):
        return lax.optimization_barrier(values)

    saved = saved_out.reshape(owners, capacity, width)
    other = 1 - half

    def part(which, first, last):
        return lax.dynamic_slice(
            saved, (which * side, 0, first), (side, capacity, last - first)
        )

    crossed = over_z(part(other, 0, HEAD).reshape(block, HEAD))
    spread = along_x(part(other, HEAD, width)).reshape(block, width - HEAD)

    def over_replicas(value):
        every = jnp.broadcast_to(value[None], (replicas, *value.shape))
        every = lax.all_to_all(every, "replica", split_axis=0, concat_axis=0, tiled=True)
        return jnp.sum(every.astype(jnp.float32), axis=0)

    pseudo = over_replicas((outer_params - local_params[0]).astype(jnp.bfloat16)) / replicas
    own_sq = jnp.sum(pseudo * pseudo).reshape(1, 1)

    own_sq = own_sq + swap_x(own_sq, 2)
    window = along_z(own_sq)
    crossed, spread, window = tie(crossed, spread, window)
    came = over_z(spread)
    window = over_replicas(window)
    crossed, window, half_then, top_logits = tie(crossed, window, half, top_logits)
    window = window + swap_x(window, 2)
    total_sq = (window + swap_x(window, 1))[0, 0]
    near = lax.dynamic_slice_in_dim(saved, half_then * side, side, 0)
    near_rows = along_x(near).reshape(block, width)
    crossed = along_x(crossed.reshape(side, capacity, HEAD)).reshape(block, HEAD)
    far_rows = [crossed, came]
    cuts = (0, HEAD, width)

    count = jnp.arange(owners, dtype=jnp.int32)
    named = [(expert_ids[:, k : k + 1] == count[None, :]).astype(jnp.bfloat16) for k in range(2)]
    row = lax.broadcasted_iota(jnp.int32, (tokens, tokens), 0)
    col = lax.broadcasted_iota(jnp.int32, (tokens, tokens), 1)
    before = jnp.dot(
        (col < row).astype(jnp.bfloat16), named[0] + named[1], preferred_element_type=jnp.float32
    )
    slot = jnp.concatenate(
        [
            expert_ids[:, k] * capacity
            + jnp.sum(before * named[k].astype(jnp.float32), axis=1).astype(jnp.int32)
            for k in range(2)
        ]
    )
    lanes = jnp.arange(block, dtype=jnp.int32)
    near_mask = (slot - half * block)[:, None] == lanes[None, :]
    far_mask = (slot - other * block)[:, None] == lanes[None, :]

    first = jax.nn.sigmoid(top_logits[:, 0] - top_logits[:, 1])
    second = 1.0 - first
    grads = out_grad.astype(jnp.float32)
    payload = jnp.concatenate(
        [
            (first[:, None] * grads).astype(jnp.bfloat16),
            (second[:, None] * grads).astype(jnp.bfloat16),
        ]
    )

    def inner(a, b):
        return lax.dot_general(
            a, b, (((1,), (1,)), ((), ())), preferred_element_type=jnp.float32
        )

    def picked(mask, rows, first, last):
        return jnp.sum(jnp.where(mask, inner(payload[:, first:last], rows), 0.0), axis=1)

    pair = picked(near_mask, near_rows, 0, width)
    for i, rows in enumerate(far_rows):
        if i == len(far_rows) - 1:
            rows, pair = lax.optimization_barrier((rows, pair))
        pair = pair + picked(far_mask, rows, cuts[i], cuts[i + 1])
    pair0, pair1 = pair[:tokens], pair[tokens:]
    both = pair0 + pair1
    logit_grad = jnp.stack([pair0 - first * both, pair1 - second * both], axis=1)

    entries = pseudo.shape[0] * owners * runs * width
    limit = 0.25 * jnp.sqrt(jnp.float32(entries) / replicas)
    scale = jnp.minimum(1.0, limit / jnp.sqrt(total_sq + 1e-06))
    clipped = scale * pseudo
    new_momentum = 0.9 * momentum + clipped
    new_outer = outer_params - 0.7 * (clipped + 0.9 * new_momentum)
    rate = jnp.take(mix_rates, fragment[0])
    mixed_params = local_params + rate * (new_outer[None] - local_params)
    return (logit_grad, new_outer, new_momentum, mixed_params)


def solution(mesh):
    in_specs = (
        P(("replica", "expert", "fsdp"), None),
        P("replica", "expert", "fsdp", None, None, None),
        P(("replica", "expert", "fsdp"), None),
        P(("replica", "expert", "fsdp"), None),
        P(("expert", "fsdp"), None),
        P("replica", ("expert", "fsdp"), None),
        P(("expert", "fsdp"), None),
        P("replica"),
        P(),
    )
    out_specs = (
        P(("replica", "expert", "fsdp"), None),
        P(("expert", "fsdp"), None),
        P(("expert", "fsdp"), None),
        P("replica", ("expert", "fsdp"), None),
    )
    return jax.shard_map(shards, mesh=mesh, in_specs=in_specs, out_specs=out_specs, check_vma=False)
```

```python
import jax
import jax.numpy as jnp
from jax import lax
from jax.sharding import PartitionSpec as P

HEAD = 2048
AXES = ("replica", "expert", "fsdp")


def shards(
    out_grad,
    saved_out,
    top_logits,
    expert_ids,
    outer_params,
    local_params,
    momentum,
    fragment,
    mix_rates,
):
    tokens, width = out_grad.shape
    replicas, owners, runs = (lax.axis_size(axis) for axis in AXES)
    capacity = saved_out.shape[4]
    side = owners // 2
    block = side * capacity
    half = lax.axis_index("expert") // side
    groups = [list(range(side)), list(range(side, owners))]
    across = [(e, (e + side) % owners) for e in range(owners)]

    def along_x(value):
        return lax.all_to_all(
            value, "expert", split_axis=0, concat_axis=0, axis_index_groups=groups, tiled=True
        )

    def over_z(value):
        return lax.ppermute(value, "expert", across)

    def swap_x(value, step):
        return lax.ppermute(value, "expert", [(e, e ^ step) for e in range(owners)])

    def place(r, z, x):
        return (r * owners + z // runs * side + x) * runs + z % runs

    depth = 2 * runs

    def along_z(value):
        return lax.ppermute(
            value,
            AXES,
            [
                (place(r, z, x), place(r, (z + r + x // 2 * replicas) % depth, x))
                for r in range(replicas)
                for z in range(depth)
                for x in range(side)
            ],
        )

    def tie(*values):
        return lax.optimization_barrier(values)

    saved = saved_out.reshape(owners, capacity, width)
    other = 1 - half

    def part(which, first, last):
        return lax.dynamic_slice(
            saved, (which * side, 0, first), (side, capacity, last - first)
        )

    crossed = over_z(part(other, 0, HEAD).reshape(block, HEAD))
    spread = along_x(part(other, HEAD, width)).reshape(block, width - HEAD)

    def over_replicas(value):
        every = jnp.broadcast_to(value[None], (replicas, *value.shape))
        every = lax.all_to_all(every, "replica", split_axis=0, concat_axis=0, tiled=True)
        return jnp.sum(every.astype(jnp.float32), axis=0)

    pseudo = (
        lax.psum((outer_params - local_params[0]).astype(jnp.bfloat16), "replica").astype(
            jnp.float32
        )
        / replicas
    )
    own_sq = jnp.sum(pseudo * pseudo).reshape(1, 1)

    own_sq = own_sq + swap_x(own_sq, 2)
    window = along_z(own_sq)
    crossed, spread, window = tie(crossed, spread, window)
    came = over_z(spread)
    window = over_replicas(window)
    crossed, window, half_then, top_logits = tie(crossed, window, half, top_logits)
    window = window + swap_x(window, 2)
    total_sq = (window + swap_x(window, 1))[0, 0]
    near = lax.dynamic_slice_in_dim(saved, half_then * side, side, 0)
    near_rows = along_x(near).reshape(block, width)
    crossed = along_x(crossed.reshape(side, capacity, HEAD)).reshape(block, HEAD)
    far_rows = [crossed, came]
    cuts = (0, HEAD, width)

    count = jnp.arange(owners, dtype=jnp.int32)
    named = [(expert_ids[:, k : k + 1] == count[None, :]).astype(jnp.bfloat16) for k in range(2)]
    row = lax.broadcasted_iota(jnp.int32, (tokens, tokens), 0)
    col = lax.broadcasted_iota(jnp.int32, (tokens, tokens), 1)
    before = jnp.dot(
        (col < row).astype(jnp.bfloat16), named[0] + named[1], preferred_element_type=jnp.float32
    )
    slot = jnp.concatenate(
        [
            expert_ids[:, k] * capacity
            + jnp.sum(before * named[k].astype(jnp.float32), axis=1).astype(jnp.int32)
            for k in range(2)
        ]
    )
    lanes = jnp.arange(block, dtype=jnp.int32)
    near_mask = (slot - half * block)[:, None] == lanes[None, :]
    far_mask = (slot - other * block)[:, None] == lanes[None, :]

    first = jax.nn.sigmoid(top_logits[:, 0] - top_logits[:, 1])
    second = 1.0 - first
    grads = out_grad.astype(jnp.float32)
    payload = jnp.concatenate(
        [
            (first[:, None] * grads).astype(jnp.bfloat16),
            (second[:, None] * grads).astype(jnp.bfloat16),
        ]
    )

    def inner(a, b):
        return lax.dot_general(
            a, b, (((1,), (1,)), ((), ())), preferred_element_type=jnp.float32
        )

    def picked(mask, rows, first, last):
        return jnp.sum(jnp.where(mask, inner(payload[:, first:last], rows), 0.0), axis=1)

    pair = picked(near_mask, near_rows, 0, width)
    for i, rows in enumerate(far_rows):
        if i == len(far_rows) - 1:
            rows, pair = lax.optimization_barrier((rows, pair))
        pair = pair + picked(far_mask, rows, cuts[i], cuts[i + 1])
    pair0, pair1 = pair[:tokens], pair[tokens:]
    both = pair0 + pair1
    logit_grad = jnp.stack([pair0 - first * both, pair1 - second * both], axis=1)

    entries = pseudo.shape[0] * owners * runs * width
    limit = 0.25 * jnp.sqrt(jnp.float32(entries) / replicas)
    scale = jnp.minimum(1.0, limit / jnp.sqrt(total_sq + 1e-06))
    clipped = scale * pseudo
    new_momentum = 0.9 * momentum + clipped
    new_outer = outer_params - 0.7 * (clipped + 0.9 * new_momentum)
    rate = jnp.take(mix_rates, fragment[0])
    mixed_params = local_params + rate * (new_outer[None] - local_params)
    return (logit_grad, new_outer, new_momentum, mixed_params)


def solution(mesh):
    in_specs = (
        P(("replica", "expert", "fsdp"), None),
        P("replica", "expert", "fsdp", None, None, None),
        P(("replica", "expert", "fsdp"), None),
        P(("replica", "expert", "fsdp"), None),
        P(("expert", "fsdp"), None),
        P("replica", ("expert", "fsdp"), None),
        P(("expert", "fsdp"), None),
        P("replica"),
        P(),
    )
    out_specs = (
        P(("replica", "expert", "fsdp"), None),
        P(("expert", "fsdp"), None),
        P(("expert", "fsdp"), None),
        P("replica", ("expert", "fsdp"), None),
    )
    return jax.shard_map(shards, mesh=mesh, in_specs=in_specs, out_specs=out_specs, check_vma=False)
```
